32 devices in a mesh: row: 4 (over y, core), col: 8 (over z, x).
Axes of the slice: x: 2, y: 2, z: 4, core: 2. Of those that a mesh axis runs over, the one named last changes fastest.
Arguments:
- factor: bfloat16 [4, 10, 512, 8, 512], P('row', None, None, 'col'), may hold values from -0.09375 to 0.09375
- dinv: bfloat16 [4, 2, 512, 512], P('row'), may hold values from -1 to 2, as said below
- rhs: float32 [4, 10, 64, 512], P('row'), may hold values from -6 to 6
Outputs:
- result: float32 [4, 10, 64, 512], P('row')
The draws below stay inside these ranges and needn't reach their ends.
Inputs may be any that keep to these rules, and one draw needn't show every extreme that they name: dinv holds the given inverses of the window's diagonal tiles; they are dense and stored apart, and factor's tiles at and below the diagonal (block row i >= 32 + j in window column j) are never read.
All inputs are finite; a program needn't handle non-finite values.
Results may differ from the reference program's by a relative error of at most 0.0028.
Values may be sent and summed in bfloat16 or wider, within the bound.
A program may use at most 64 MiB of HBM per device.

```python
import math
import jax
import jax.numpy as jnp
from jax import lax

B = 512
NRHS = 64
LEAD = 8
GROWS = 4
NCW = 8
DIAG = 2
TR = 10


def draw_dinv(key, part):
    key = jax.random.fold_in(key, 7)
    key_diag, key_off = jax.random.split(key)
    diagonal = jax.random.uniform(key_diag, (GROWS, DIAG, B), jnp.float32, 0.5, 1.5)
    offdiag = jax.random.normal(key_off, (GROWS, DIAG, B, B), jnp.float32) * (0.3 / math.sqrt(B))
    identity = jnp.eye(B, dtype=jnp.float32)
    return (offdiag + identity * diagonal[..., None]).astype(jnp.bfloat16)


def steps_of(stream_key, shape, shards, low, high):
    factor_of = 1.0
    for dim, blocks in shards:
        draws = jax.random.uniform(jax.random.fold_in(jax.random.fold_in(stream_key, 6), dim), (blocks,), jnp.float32, low / len(shards), high / len(shards))
        factor_of = factor_of * jnp.repeat(jnp.exp(draws), shape[dim] // blocks).reshape((-1,) + (1,) * (len(shape) - 1 - dim))
    return factor_of


def noise(rng, shape, deviation, most, pieces=(), kind=jnp.bfloat16):
    gain = steps_of(rng, shape, pieces, -0.22, 0.18) if pieces else 1.0
    result = jax.random.normal(rng, shape, jnp.float32) * deviation * gain
    return jnp.minimum(jnp.maximum(result, -most), most).astype(kind)


def setup_inputs(seed: int = 0) -> dict:
    key_list = jax.random.split(jax.random.key(seed), 4)
    factor = noise(key_list[0], (GROWS, TR, B, NCW, B), (B * NCW) ** -0.5, 0.09375, ((0, 4), (3, 8)))
    dinv = draw_dinv(jax.random.fold_in(key_list[3], 71), 0)
    rhs = noise(key_list[2], (GROWS, TR, NRHS, B), 1.0, 6.0, ((0, 4),), jnp.float32)
    return {"factor": factor, "dinv": dinv, "rhs": rhs}


def reference(factor, dinv, rhs):
    offset = LEAD * GROWS
    total_rows = TR * GROWS
    rhs_glob = jnp.transpose(rhs, (1, 0, 2, 3)).reshape(total_rows, NRHS, B)
    fac_glob = jnp.transpose(factor, (1, 0, 2, 3, 4)).reshape(total_rows, B, NCW, B)
    inv_glob = jnp.transpose(dinv, (1, 0, 2, 3)).reshape(NCW, B, B)
    block_ids = jnp.arange(total_rows, dtype=jnp.int32)
    partials = jnp.zeros((total_rows, NRHS, B), jnp.float32)
    results = rhs_glob
    for column in range(NCW - 1, -1, -1):
        target = offset + column
        y_block = rhs_glob[target] - partials[target]
        x_block = jnp.dot(y_block, inv_glob[column].astype(jnp.float32).T, precision=lax.Precision.HIGHEST, preferred_element_type=jnp.float32)
        results = results.at[target].set(x_block)
        x_round = x_block.astype(jnp.bfloat16)
        products = jnp.einsum('nb,iab->ina', x_round.astype(jnp.float32), fac_glob[:, :, column, :].astype(jnp.float32))
        partials = partials + jnp.where((block_ids < target)[:, None, None], products, jnp.float32(0.0))
    results = results.at[:offset].set(rhs_glob[:offset] - partials[:offset])
    return jnp.transpose(results.reshape(TR, GROWS, NRHS, B), (1, 0, 2, 3))
```

```python
import functools

import jax
import jax.numpy as jnp
from jax import lax
from jax.experimental import pallas as pl
from jax.experimental.pallas import tpu as pltpu
from jax.sharding import PartitionSpec as P

MESH = pl.DeviceIdType.MESH
F32 = jnp.float32
BF16 = jnp.bfloat16


def dot_nt(a, b):
    return lax.dot_general(a, b, (((1,), (1,)), ((), ())), preferred_element_type=F32)


def times_inverse(y, inv):
    n = y.shape[0]
    high = y.astype(BF16)
    low = (y - high.astype(F32)).astype(BF16)
    both = dot_nt(jnp.concatenate([high, low], axis=0), inv)
    return both[:n] + both[n:]


def kernel(
    grid_rows, grid_cols, lead, diag, nrhs, pieces,
    factor_in, inv_in, rhs_in, out,
    factor, inv, rhs, held, parts, part_out, lead_out, lead_in, sums, solved, y_acc,
    load_sem, x_send, x_recv, p_send, p_recv, l_send, l_recv, s_send, s_recv, r_send, r_recv,
):
    r = lax.axis_index("row")
    c = lax.axis_index("col")
    last = grid_cols - 1
    last_row, last_slot = last % grid_rows, last // grid_rows
    loads = [
        pltpu.make_async_copy(inv_in, inv, load_sem.at[0]),
        pltpu.make_async_copy(rhs_in, rhs, load_sem.at[1]),
        pltpu.make_async_copy(
            factor_in.at[pl.ds(lead, diag)], factor.at[pl.ds(lead, diag)], load_sem.at[2]
        ),
        pltpu.make_async_copy(
            factor_in.at[pl.ds(0, lead)], factor.at[pl.ds(0, lead)], load_sem.at[3]
        ),
    ]
    for load in loads:
        load.start()

    barrier = pltpu.get_barrier_semaphore()
    for step in range(1, grid_cols):
        pl.semaphore_signal(
            barrier, inc=1, device_id=(r, lax.rem(c + step, grid_cols)), device_id_type=MESH
        )
    for dr in range(1, grid_rows):
        for dc in (grid_cols - 1, 0, 1):
            pl.semaphore_signal(
                barrier,
                inc=1,
                device_id=(lax.rem(r + dr, grid_rows), lax.rem(c + dc, grid_cols)),
                device_id_type=MESH,
            )
    pl.semaphore_wait(barrier, grid_cols - 1 + 3 * (grid_rows - 1))

    def x_copy(src, row, col):
        return pltpu.make_async_remote_copy(
            src_ref=src, dst_ref=held, send_sem=x_send.at[row], recv_sem=x_recv,
            device_id=(row, col), device_id_type=MESH,
        )

    def part_copy(d, src_col, dst_col):
        return pltpu.make_async_remote_copy(
            src_ref=part_out.at[d], dst_ref=parts.at[src_col], send_sem=p_send.at[d],
            recv_sem=p_recv.at[src_col], device_id=(r, dst_col), device_id_type=MESH,
        )

    def lead_copy(piece, src_col):
        return pltpu.make_async_remote_copy(
            src_ref=lead_out.at[piece], dst_ref=lead_in.at[src_col], send_sem=l_send.at[piece],
            recv_sem=l_recv.at[src_col], device_id=(r, piece), device_id_type=MESH,
        )

    def sum_copy(src_col, dst_col):
        return pltpu.make_async_remote_copy(
            src_ref=sums.at[src_col], dst_ref=sums.at[src_col], send_sem=s_send.at[dst_col],
            recv_sem=s_recv.at[src_col], device_id=(r, dst_col), device_id_type=MESH,
        )

    def solved_copy(d, dst_col):
        return pltpu.make_async_remote_copy(
            src_ref=solved.at[d], dst_ref=solved.at[d], send_sem=r_send.at[dst_col],
            recv_sem=r_recv.at[d], device_id=(r, dst_col), device_id_type=MESH,
        )

    first_owner = jnp.logical_and(r == last_row, c == last)
    loads[0].wait()
    loads[1].wait()

    @pl.when(r == last_row)
    def _():
        solved[last_slot] = times_inverse(rhs[lead + last_slot], inv[last_slot]).astype(BF16)

    @pl.when(first_owner)
    def _():
        for dr in range(1, grid_rows):
            x_copy(solved.at[last_slot], (last_row + dr) % grid_rows, last).start()
        held[...] = solved[last_slot]

    loads[2].wait()

    k = c - 1
    solver = jnp.logical_and(c >= 1, r == lax.rem(k + grid_rows, grid_rows))
    kd = lax.div(jnp.maximum(k, 0), grid_rows)

    @pl.when(solver)
    def _():
        y_acc[...] = rhs[lead + kd]

        def add(step, carry):
            src = last - step
            part_copy(0, src, c).wait_recv()
            y_acc[...] -= parts[src].astype(F32)
            return carry

        lax.fori_loop(0, jnp.maximum(last - c - 1, 0), add, 0)

    @pl.when(jnp.logical_not(first_owner))
    def _():
        x_copy(held, r, c).wait_recv()

    @pl.when(solver)
    def _():
        y_acc[...] -= dot_nt(held[...], factor[lead + kd])

        @pl.when(c + 1 <= last)
        def _():
            src = jnp.minimum(c + 1, last)
            part_copy(0, src, c).wait_recv()
            y_acc[...] -= parts[src].astype(F32)

        solved[kd] = times_inverse(y_acc[...], inv[kd]).astype(BF16)
        for dr in range(1, grid_rows + 1):
            row = lax.rem(r - dr + 2 * grid_rows, grid_rows)
            x_copy(solved.at[kd], row, k).start()

    for d in reversed(range(diag)):
        block = d * grid_rows + r

        @pl.when(block < k)
        def _():
            part_out[d] = dot_nt(held[...], factor[lead + d]).astype(BF16)
            part_copy(d, c, block + 1).start()

    loads[3].wait()
    per_block = pieces // lead
    rows = nrhs // per_block

    def lead_step(t, carry):
        product = dot_nt(held[...], factor[t]).astype(BF16)
        for q in range(per_block):
            piece = t * per_block + q
            lead_out[piece] = product[q * rows : (q + 1) * rows]

            @pl.when(piece != c)
            def _():
                lead_copy(piece, c).start()

        return carry

    lax.fori_loop(0, lead, lead_step, 0)

    @pl.when(solver)
    def _():
        def send(step, carry):
            solved_copy(kd, lax.rem(c + step, grid_cols)).start()
            return carry

        lax.fori_loop(1, grid_cols, send, 0)

    def add_lead(step, total):
        src = last - step

        @pl.when(src != c)
        def _():
            lead_copy(c, src).wait_recv()

        @pl.when(src == c)
        def _():
            lead_in[src] = lead_out[c]

        return total + lead_in[src].astype(F32)

    total = lax.fori_loop(0, grid_cols, add_lead, jnp.zeros(lead_in.shape[1:], F32))
    sums[c] = total.astype(BF16)

    def send_sum(step, carry):
        sum_copy(c, lax.rem(c + step, grid_cols)).start()
        return carry

    lax.fori_loop(1, grid_cols, send_sum, 0)

    for d in range(diag):
        block = d * grid_rows + r

        @pl.when(jnp.logical_and(block != last, block + 1 != c))
        def _():
            solved_copy(d, c).wait_recv()

        out[lead + d] = solved[d]

    def wait_sum(step, carry):
        sum_copy(lax.rem(c + step, grid_cols), c).wait_recv()
        return carry

    lax.fori_loop(1, grid_cols, wait_sum, 0)
    for t in range(lead):
        for q in range(per_block):
            out[t, q * rows : (q + 1) * rows] = sums[t * per_block + q]

    @pl.when(first_owner)
    def _():
        for dr in range(1, grid_rows):
            x_copy(solved.at[last_slot], (last_row + dr) % grid_rows, last).wait_send()

    @pl.when(solver)
    def _():
        for row in range(grid_rows):
            x_copy(solved.at[kd], row, k).wait_send()

        def sent(step, carry):
            solved_copy(kd, lax.rem(c + step, grid_cols)).wait_send()
            return carry

        lax.fori_loop(1, grid_cols, sent, 0)

    for d in range(diag):
        block = d * grid_rows + r

        @pl.when(block < k)
        def _():
            part_copy(d, c, block + 1).wait_send()

    def all_sent(step, carry):
        other = lax.rem(c + step, grid_cols)
        lead_copy(other, c).wait_send()
        sum_copy(c, other).wait_send()
        return carry

    lax.fori_loop(1, grid_cols, all_sent, 0)


def shards(factor, dinv, rhs):
    grid_rows = lax.axis_size("row")
    grid_cols = lax.axis_size("col")
    tiles = factor.reshape(factor.shape[1], factor.shape[2], factor.shape[4])
    inverse = dinv[0]
    local_rhs = rhs[0]
    held_rows, nrhs, order = local_rhs.shape
    diag = inverse.shape[0]
    lead = held_rows - diag
    pieces = grid_cols
    assert pieces % lead == 0 and (lead * nrhs) % (16 * pieces) == 0
    rows = lead * nrhs // pieces
    dma = pltpu.SemaphoreType.DMA
    update = pl.pallas_call(
        functools.partial(kernel, grid_rows, grid_cols, lead, diag, nrhs, pieces),
        out_shape=jax.ShapeDtypeStruct((held_rows, nrhs, order), BF16),
        in_specs=[pl.BlockSpec(memory_space=pl.ANY)] * 3,
        out_specs=pl.BlockSpec(memory_space=pltpu.VMEM),
        scratch_shapes=[
            pltpu.VMEM(tiles.shape, BF16),
            pltpu.VMEM(inverse.shape, BF16),
            pltpu.VMEM(local_rhs.shape, F32),
            pltpu.VMEM((nrhs, order), BF16),
            pltpu.VMEM((grid_cols, nrhs, order), BF16),
            pltpu.VMEM((diag, nrhs, order), BF16),
            pltpu.VMEM((pieces, rows, order), BF16),
            pltpu.VMEM((grid_cols, rows, order), BF16),
            pltpu.VMEM((pieces, rows, order), BF16),
            pltpu.VMEM((diag, nrhs, order), BF16),
            pltpu.VMEM((nrhs, order), F32),
            dma((4,)),
            dma((grid_rows,)),
            dma,
            dma((diag,)),
            dma((grid_cols,)),
            dma((pieces,)),
            dma((grid_cols,)),
            dma((grid_cols,)),
            dma((grid_cols,)),
            dma((grid_cols,)),
            dma((diag,)),
        ],
        compiler_params=pltpu.CompilerParams(
            collective_id=0, has_side_effects=True, vmem_limit_bytes=48 * 1024 * 1024
        ),
        cost_estimate=pl.CostEstimate(
            flops=2 * held_rows * nrhs * order * order,
            bytes_accessed=2 * held_rows * order * order,
            transcendentals=0,
        ),
    )(tiles, inverse, local_rhs).astype(F32)
    leading = lax.broadcasted_iota(jnp.int32, (held_rows, 1, 1), 0) < lead
    return jnp.where(leading, local_rhs - update, update)[None]


def solution(mesh):
    in_specs = (
        P("row", None, None, "col", None),
        P("row", None, None, None),
        P("row", None, None, None),
    )
    out_specs = P("row", None, None, None)
    return jax.shard_map(shards, mesh=mesh, in_specs=in_specs, out_specs=out_specs, check_vma=False)
```

```python
import functools

import jax
import jax.numpy as jnp
from jax import lax
from jax.experimental import pallas as pl
from jax.experimental.pallas import tpu as pltpu
from jax.sharding import PartitionSpec as P

MESH = pl.DeviceIdType.MESH
F32 = jnp.float32
BF16 = jnp.bfloat16


def dot_nt(a, b):
    return lax.dot_general(a, b, (((1,), (1,)), ((), ())), preferred_element_type=F32)


def times_inverse(y, inv):
    n = y.shape[0]
    high = y.astype(BF16)
    low = (y - high.astype(F32)).astype(BF16)
    both = dot_nt(jnp.concatenate([high, low], axis=0), inv)
    return both[:n] + both[n:]


def kernel(
    grid_rows, grid_cols, lead, diag, nrhs, pieces,
    factor_in, inv_in, rhs_in, out,
    factor, inv, rhs, held, parts, part_out, lead_out, lead_in, sums, solved, y_acc,
    held_two, tile_two, pair_in, q_recv, h_recv, t_send, t_recv, load_sem, x_send, x_recv, p_send, p_recv, l_send, l_recv, s_send, s_recv, r_send, r_recv, relay_send,
):
    r = lax.axis_index("row")
    c = lax.axis_index("col")
    last = grid_cols - 1
    last_row, last_slot = last % grid_rows, last // grid_rows
    loads = [
        pltpu.make_async_copy(inv_in, inv, load_sem.at[0]),
        pltpu.make_async_copy(rhs_in, rhs, load_sem.at[1]),
        pltpu.make_async_copy(
            factor_in.at[pl.ds(lead, diag)], factor.at[pl.ds(lead, diag)], load_sem.at[2]
        ),
        pltpu.make_async_copy(
            factor_in.at[pl.ds(0, lead)], factor.at[pl.ds(0, lead)], load_sem.at[3]
        ),
    ]
    for load in loads:
        load.start()

    barrier = pltpu.get_barrier_semaphore()
    for step in range(1, grid_cols):
        pl.semaphore_signal(
            barrier, inc=1, device_id=(r, lax.rem(c + step, grid_cols)), device_id_type=MESH
        )
    for dr in range(1, grid_rows):
        for dc in (grid_cols - 2, grid_cols - 1, 0, 1, 2):
            pl.semaphore_signal(
                barrier,
                inc=1,
                device_id=(lax.rem(r + dr, grid_rows), lax.rem(c + dc, grid_cols)),
                device_id_type=MESH,
            )
    pl.semaphore_wait(barrier, grid_cols - 1 + 5 * (grid_rows - 1))

    chips = grid_rows // 2

    two_row = jnp.logical_and(c >= 2, r == lax.rem(c - 2 + grid_rows, grid_rows))

    def two_copy():
        block = lax.div(jnp.maximum(c - 2, 0), grid_rows)
        return pltpu.make_async_remote_copy(
            src_ref=factor_in.at[lead + block], dst_ref=tile_two, send_sem=t_send,
            recv_sem=t_recv, device_id=(r, jnp.maximum(c - 1, 0)), device_id_type=MESH,
        )

    @pl.when(two_row)
    def _():
        two_copy().start()

    def x_copy(src, row, col, sem):
        return pltpu.make_async_remote_copy(
            src_ref=src, dst_ref=held, send_sem=x_send.at[sem], recv_sem=x_recv,
            device_id=(row, col), device_id_type=MESH,
        )

    def two_x_copy(src, row, col):
        return pltpu.make_async_remote_copy(
            src_ref=src, dst_ref=held_two, send_sem=x_send.at[chips], recv_sem=h_recv,
            device_id=(row, col), device_id_type=MESH,
        )

    def x_copies(src, column, row, act):
        after = lax.rem(row + grid_rows - 1, grid_rows)
        act(x_copy(src, after, column, 0))

        @pl.when(column >= 2)
        def _():
            act(
                two_x_copy(
                    src, lax.rem(row + grid_rows - 2, grid_rows), jnp.maximum(column - 1, 0)
                )
            )

        for step in range(1, chips):
            chip = lax.rem(lax.div(after, 2) + step, chips)
            act(x_copy(src, 2 * chip + 1, column, step))

    def part_copy(d, src_col, dst_col):
        return pltpu.make_async_remote_copy(
            src_ref=part_out.at[d], dst_ref=parts.at[src_col], send_sem=p_send.at[d],
            recv_sem=p_recv.at[src_col], device_id=(r, dst_col), device_id_type=MESH,
        )

    def lead_copy(piece, src_col):
        return pltpu.make_async_remote_copy(
            src_ref=lead_out.at[piece], dst_ref=lead_in.at[src_col], send_sem=l_send.at[piece],
            recv_sem=l_recv.at[src_col], device_id=(r, piece), device_id_type=MESH,
        )

    def sum_copy(src_col, dst_col):
        return pltpu.make_async_remote_copy(
            src_ref=sums.at[src_col], dst_ref=sums.at[src_col], send_sem=s_send.at[dst_col],
            recv_sem=s_recv.at[src_col], device_id=(r, dst_col), device_id_type=MESH,
        )

    def solved_copy(d, dst_col, relayed=False):
        return pltpu.make_async_remote_copy(
            src_ref=solved.at[d], dst_ref=solved.at[d],
            send_sem=relay_send.at[d] if relayed else r_send.at[dst_col],
            recv_sem=r_recv.at[d], device_id=(r, dst_col), device_id_type=MESH,
        )

    first_owner = jnp.logical_and(r == last_row, c == last)
    loads[0].wait()
    loads[1].wait()

    @pl.when(r == last_row)
    def _():
        solved[last_slot] = times_inverse(rhs[lead + last_slot], inv[last_slot]).astype(BF16)

    @pl.when(first_owner)
    def _():
        x_copies(solved.at[last_slot], last, last_row, lambda copy: copy.start())
        held[...] = solved[last_slot]

    loads[2].wait()

    k = c - 1
    solver = jnp.logical_and(c >= 1, r == lax.rem(k + grid_rows, grid_rows))
    kd = lax.div(jnp.maximum(k, 0), grid_rows)

    @pl.when(solver)
    def _():
        y_acc[...] = rhs[lead + kd]

        def add(step, carry):
            src = last - step
            part_copy(0, src, c).wait_recv()
            y_acc[...] -= parts[src]
            return carry

        lax.fori_loop(0, jnp.maximum(last - c - 1, 0), add, 0)

        @pl.when(c + 1 <= last)
        def _():
            two_copy().wait_recv()
            two_x_copy(held_two, r, c).wait_recv()
            y_acc[...] -= dot_nt(held_two[...], tile_two[...])

    @pl.when(jnp.logical_not(first_owner))
    def _():
        x_copy(held, r, c, 0).wait_recv()

    after = lax.rem(c - 1 + grid_rows, grid_rows)
    lead_of_chip = jnp.where(
        lax.div(r, 2) == lax.div(after, 2), r == after, lax.rem(r, 2) == 1
    )
    relay = jnp.logical_and(
        lead_of_chip, jnp.logical_not(jnp.logical_and(c == last, lax.div(r, 2) == last_row // 2))
    )
    sibling = r + 1 - 2 * lax.rem(r, 2)

    @pl.when(relay)
    def _():
        x_copy(held, sibling, c, chips + 1).start()

    @pl.when(solver)
    def _():
        y_acc[...] -= dot_nt(held[...], factor[lead + kd])
        solved[kd] = times_inverse(y_acc[...], inv[kd]).astype(BF16)
        x_copies(solved.at[kd], k, r, lambda copy: copy.start())

    for d in reversed(range(diag)):
        block = d * grid_rows + r

        @pl.when(block < k - 1)
        def _():
            part_out[d] = dot_nt(held[...], factor[lead + d])
            part_copy(d, c, block + 1).start()

    loads[3].wait()
    per_block = pieces // lead
    pair = c + 1 - 2 * lax.rem(c, 2)
    parity = lax.rem(c, 2)
    half = grid_cols // 2
    rows = nrhs // per_block
    early = c >= 2

    def pair_copy(piece):
        return pltpu.make_async_remote_copy(
            src_ref=lead_out.at[piece], dst_ref=pair_in.at[lax.div(piece, 2)],
            send_sem=l_send.at[piece], recv_sem=q_recv.at[lax.div(piece, 2)],
            device_id=(r, pair), device_id_type=MESH,
        )

    def lead_step(t, carry):
        product = dot_nt(held[...], factor[t]).astype(BF16)
        for q in range(per_block):
            piece = t * per_block + q
            lead_out[piece] = product[q * rows : (q + 1) * rows]

            @pl.when(jnp.logical_and(early, lax.rem(piece, 2) != parity))
            def _():
                pair_copy(piece).start()

            @pl.when(jnp.logical_and(jnp.logical_not(early), piece != c))
            def _():
                lead_copy(piece, c).start()

        return carry

    lax.fori_loop(0, lead, lead_step, 0)

    @pl.when(solver)
    def _():
        def send(step, carry):
            solved_copy(kd, lax.rem(c + 2 * step, grid_cols)).start()
            return carry

        solved_copy(kd, pair).start()
        lax.fori_loop(1, half, send, 0)

    @pl.when(early)
    def _():
        def join(m, carry):
            piece = 2 * m + parity
            pair_copy(piece).wait_recv()
            lead_out[piece] = (
                lead_out[piece].astype(F32) + pair_in[m].astype(F32)
            ).astype(BF16)

            @pl.when(piece != c)
            def _():
                lead_copy(piece, c).start()

            return carry

        lax.fori_loop(0, half, join, 0)

    def add_lead(step, total):
        src = jnp.where(step < half - 1, 2 * (half - 1 - step) + parity, half - step)

        @pl.when(src != c)
        def _():
            lead_copy(c, src).wait_recv()

        @pl.when(src == c)
        def _():
            lead_in[src] = lead_out[c]

        return total + lead_in[src].astype(F32)

    total = lax.fori_loop(0, half + 1, add_lead, jnp.zeros(lead_in.shape[1:], F32))
    sums[c] = total.astype(BF16)

    def send_sum(step, carry):
        sum_copy(c, lax.rem(c + step, grid_cols)).start()
        return carry

    lax.fori_loop(1, grid_cols, send_sum, 0)

    for d in range(diag):
        block = d * grid_rows + r

        @pl.when(jnp.logical_and(block != last, block + 1 != c))
        def _():
            solved_copy(d, c).wait_recv()

            @pl.when(lax.rem(block + 1, 2) == parity)
            def _():
                solved_copy(d, pair, True).start()

        out[lead + d] = solved[d]

    def wait_sum(step, carry):
        sum_copy(lax.rem(c + step, grid_cols), c).wait_recv()
        return carry

    lax.fori_loop(1, grid_cols, wait_sum, 0)
    for t in range(lead):
        for q in range(per_block):
            out[t, q * rows : (q + 1) * rows] = sums[t * per_block + q]

    @pl.when(two_row)
    def _():
        two_copy().wait_send()

    @pl.when(relay)
    def _():
        x_copy(held, sibling, c, chips + 1).wait_send()

    @pl.when(first_owner)
    def _():
        x_copies(solved.at[last_slot], last, last_row, lambda copy: copy.wait_send())

    @pl.when(solver)
    def _():
        x_copies(solved.at[kd], k, r, lambda copy: copy.wait_send())

        def sent(step, carry):
            solved_copy(kd, lax.rem(c + 2 * step, grid_cols)).wait_send()
            return carry

        solved_copy(kd, pair).wait_send()
        lax.fori_loop(1, half, sent, 0)

    for d in range(diag):
        block = d * grid_rows + r
        other = jnp.logical_and(block != last, block + 1 != c)

        @pl.when(jnp.logical_and(other, lax.rem(block + 1, 2) == parity))
        def _():
            solved_copy(d, pair, True).wait_send()

    for d in range(diag):
        block = d * grid_rows + r

        @pl.when(block < k - 1)
        def _():
            part_copy(d, c, block + 1).wait_send()

    def all_sent(step, carry):
        other = lax.rem(c + step, grid_cols)
        lead_copy(other, c).wait_send()
        sum_copy(c, other).wait_send()
        return carry

    lax.fori_loop(1, grid_cols, all_sent, 0)


def shards(factor, dinv, rhs):
    grid_rows = lax.axis_size("row")
    grid_cols = lax.axis_size("col")
    tiles = factor.reshape(factor.shape[1], factor.shape[2], factor.shape[4])
    inverse = dinv[0]
    local_rhs = rhs[0]
    held_rows, nrhs, order = local_rhs.shape
    diag = inverse.shape[0]
    lead = held_rows - diag
    pieces = grid_cols
    assert grid_rows % 2 == 0 and grid_cols % grid_rows == 0 and grid_cols >= 5
    assert grid_cols % 2 == 0
    assert pieces % lead == 0 and (lead * nrhs) % (16 * pieces) == 0
    rows = lead * nrhs // pieces
    dma = pltpu.SemaphoreType.DMA
    update = pl.pallas_call(
        functools.partial(kernel, grid_rows, grid_cols, lead, diag, nrhs, pieces),
        out_shape=jax.ShapeDtypeStruct((held_rows, nrhs, order), BF16),
        in_specs=[pl.BlockSpec(memory_space=pl.ANY)] * 3,
        out_specs=pl.BlockSpec(memory_space=pltpu.VMEM),
        scratch_shapes=[
            pltpu.VMEM(tiles.shape, BF16),
            pltpu.VMEM(inverse.shape, BF16),
            pltpu.VMEM(local_rhs.shape, F32),
            pltpu.VMEM((nrhs, order), BF16),
            pltpu.VMEM((grid_cols, nrhs, order), F32),
            pltpu.VMEM((diag, nrhs, order), F32),
            pltpu.VMEM((pieces, rows, order), BF16),
            pltpu.VMEM((grid_cols, rows, order), BF16),
            pltpu.VMEM((pieces, rows, order), BF16),
            pltpu.VMEM((diag, nrhs, order), BF16),
            pltpu.VMEM((nrhs, order), F32),
            pltpu.VMEM((nrhs, order), BF16),
            pltpu.VMEM((order, order), BF16),
            pltpu.VMEM((grid_cols // 2, rows, order), BF16),
            dma((grid_cols // 2,)),
            dma,
            dma,
            dma,
            dma((4,)),
            dma((grid_rows // 2 + 2,)),
            dma,
            dma((diag,)),
            dma((grid_cols,)),
            dma((pieces,)),
            dma((grid_cols,)),
            dma((grid_cols,)),
            dma((grid_cols,)),
            dma((grid_cols,)),
            dma((diag,)),
            dma((diag,)),
        ],
        compiler_params=pltpu.CompilerParams(
            collective_id=0, has_side_effects=True, vmem_limit_bytes=60 * 1024 * 1024
        ),
        cost_estimate=pl.CostEstimate(
            flops=2 * held_rows * nrhs * order * order,
            bytes_accessed=2 * held_rows * order * order,
            transcendentals=0,
        ),
    )(tiles, inverse, local_rhs).astype(F32)
    leading = lax.broadcasted_iota(jnp.int32, (held_rows, 1, 1), 0) < lead
    return jnp.where(leading, local_rhs - update, update)[None]


def solution(mesh):
    in_specs = (
        P("row", None, None, "col", None),
        P("row", None, None, None),
        P("row", None, None, None),
    )
    out_specs = P("row", None, None, None)
    return jax.shard_map(shards, mesh=mesh, in_specs=in_specs, out_specs=out_specs, check_vma=False)
```
